32 devices in a mesh: dp: 8 (over z, x), outer: 4 (over y, core).
Axes of the slice: x: 2, y: 2, z: 4, core: 2. Of those that a mesh axis runs over, the one named last changes fastest.
Arguments:
- image_embeds: bfloat16 [4, 2048, 1152], P('outer', 'dp'), may hold values from -6 to 6
- text_features: bfloat16 [4, 2048, 1152], P('outer', 'dp'), may hold values from -92 to 92
- projection: bfloat16 [1152, 1152], replicated, may hold values from -0.1875 to 0.1875
- pair_step: int32 [4, 2048], P('outer'), may hold values from 0 to 5
- pair_col: int32 [4, 2048], P('outer'), may hold values from 0 to 255
Outputs:
- grad_text: bfloat16 [4, 2048, 1152], P('outer', 'dp')
- grad_proj: float32 [1152, 1152], P('dp', 'outer')
The draws below stay inside these ranges and needn't reach their ends.
Inputs may be any that keep to these rules, and one draw needn't show every extreme that they name: pair_step of image row i in shard a points at text shard a - pair_step + 2 of the same group.
All inputs are finite; a program needn't handle non-finite values.
Results may differ from the reference program's by a relative error of at most 0.02.
Values may be sent and summed in bfloat16 or wider, within the bound.
A program may use at most 64 MiB of HBM per device.

```python
import math
import jax
import jax.numpy as jnp
from jax import lax

D = 1152
E = 1152
B_DEV = 256
STEPS = 6
LEAD = 2
ROWS = 2048
N_DP = 8
N_OUTER = 4


def draw_text_features(key, part):
    key = jax.random.fold_in(key, 11)
    first_key, second_key = jax.random.split(key, 2)
    position = jnp.arange(D, dtype=jnp.float32) / D
    scales = 10.0 ** position * jnp.exp(jax.random.uniform(second_key, (D,), jnp.float32, -0.3, 0.3))
    values = jnp.clip(jax.random.normal(first_key, (N_OUTER, ROWS, D), jnp.float32), -6.0, 6.0) * scales
    return values.astype(jnp.bfloat16)


def plant(drawn, own_key, least, high):
    longest = drawn.shape.index(max(drawn.shape))
    spots = []
    for shift in (0, 1):
        where = [jax.random.randint(jax.random.fold_in(own_key, axis), (), 0, length) for axis, length in enumerate(drawn.shape)]
        where[longest] = (where[longest] + shift) % drawn.shape[longest]
        spots.append(tuple(where))
    return drawn.at[spots[0]].set(least).at[spots[1]].set(high)


def shard_levels(rng, dims, cuts, smallest, high):
    def one(axis_at, blocks):
        steps = jax.random.uniform(jax.random.fold_in(jax.random.fold_in(rng, 6), axis_at), (blocks,), jnp.float32, smallest / len(cuts), high / len(cuts))
        return jnp.repeat(jnp.exp(steps), dims[axis_at] // blocks).reshape((-1,) + (1,) * (len(dims) - axis_at - 1))

    level = one(*cuts[0])
    for cut in cuts[1:]:
        level = level * one(*cut)
    return level


def scatter_about(stream_key, shape, deviation, bound, shards=(), held_as=jnp.bfloat16):
    values = jax.random.normal(stream_key, shape, jnp.float32) * deviation
    if len(shards) > 0:
        values = shard_levels(stream_key, shape, shards, -0.22, 0.18) * values
    return jnp.clip(values, min=-bound, max=bound).astype(held_as)


def setup_inputs(seed: int = 0) -> dict:
    key_list = jax.random.split(jax.random.key(seed), 6)
    return {
        "image_embeds": scatter_about(key_list[0], (N_OUTER, ROWS, E), 1.0, 6.0, ((0, 4), (1, 8))),
        "text_features": draw_text_features(jax.random.fold_in(key_list[5], 71), 0),
        "projection": scatter_about(key_list[2], (D, E), D ** -0.5, 0.1875),
        "pair_step": plant(jax.random.randint(key_list[3], (N_OUTER, ROWS), 0, STEPS), jax.random.fold_in(key_list[3], 1), 0, STEPS - 1).astype(jnp.int32),
        "pair_col": plant(jax.random.randint(key_list[4], (N_OUTER, ROWS), 0, B_DEV), jax.random.fold_in(key_list[4], 1), 0, B_DEV - 1).astype(jnp.int32),
    }


LOGIT_SCALE = 10.0
LOGIT_BIAS = -3.0
LOSS_SCALE = 256.0
EPSILON = 1e-06

def unit_rows(values):
    values = values.astype(jnp.float32)
    inverse = lax.rsqrt(lax.optimization_barrier(jnp.sum(values * values, axis=-1, keepdims=True)) + EPSILON)
    return (values * inverse, inverse)

def reference(image_embeds, text_features, projection, pair_step, pair_col):
    stack_pos = jnp.repeat(jnp.arange(STEPS, dtype=jnp.int32), B_DEV)
    offsets = jnp.arange(STEPS, dtype=jnp.int32) - LEAD
    columns = lax.broadcasted_iota(jnp.int32, (STEPS * B_DEV, B_DEV), 1)
    grad_sum = jnp.zeros((D, E), jnp.float32)
    grads = []
    for group in range(N_OUTER):
        unit_img = unit_rows(image_embeds[group])[0].astype(jnp.bfloat16)
        features = text_features[group]
        hidden = jnp.dot(features, projection, preferred_element_type=jnp.float32)
        unit_text, inverse_norm = unit_rows(hidden)
        text_units = unit_text.astype(jnp.bfloat16)
        img_blocks = unit_img.reshape(N_DP, B_DEV, E)
        step_blocks = pair_step[group].reshape(N_DP, B_DEV)
        col_blocks = pair_col[group].reshape(N_DP, B_DEV)

        def one_shard(shard):
            shard_ids = (shard + offsets + N_DP) % N_DP
            images = img_blocks[shard_ids].reshape(STEPS * B_DEV, E)
            step_ids = step_blocks[shard_ids].reshape(STEPS * B_DEV)
            col_ids = col_blocks[shard_ids].reshape(STEPS * B_DEV)
            texts = lax.dynamic_slice_in_dim(text_units, (shard * B_DEV).astype(jnp.int32), B_DEV)
            logits = LOGIT_SCALE * jnp.dot(images, texts.T, preferred_element_type=jnp.float32) + LOGIT_BIAS
            positive = (step_ids == stack_pos)[:, None] & (col_ids[:, None] == columns)
            target = jnp.where(positive, 1.0, -1.0).astype(jnp.float32)
            weights = (-LOSS_SCALE * LOGIT_SCALE * target * jax.nn.sigmoid(-target * logits)).astype(jnp.bfloat16)
            return jnp.dot(weights.T, images, preferred_element_type=jnp.float32)
        unit_grad = lax.map(one_shard, jnp.arange(N_DP, dtype=jnp.int32)).reshape(ROWS, E)
        radial = lax.optimization_barrier(jnp.sum(unit_text * unit_grad, axis=-1, keepdims=True))
        hidden_grad = (inverse_norm * (unit_grad - unit_text * radial)).astype(jnp.bfloat16)
        grads.append(jnp.dot(hidden_grad, projection.T, preferred_element_type=jnp.float32).astype(jnp.bfloat16))

        def add_partial(carry, pieces):
            block_sum = jnp.dot(pieces[0].T, pieces[1], preferred_element_type=jnp.float32)
            rounded = lax.optimization_barrier(block_sum.astype(jnp.bfloat16)).astype(jnp.float32)
            return (carry + rounded, None)
        grad_sum, _ = lax.scan(add_partial, grad_sum, (features.reshape(N_DP, B_DEV, D), hidden_grad.reshape(N_DP, B_DEV, E)))
    grad_norm = jnp.sqrt(jnp.sum(grad_sum * grad_sum))
    factor = jnp.minimum(1.0, math.sqrt(D * E) / grad_norm)
    return (jnp.stack(grads), grad_sum * factor)
```

```python
import math

import jax
import jax.numpy as jnp
from jax import lax
from jax.experimental import pallas as pl
from jax.experimental.pallas import tpu as pltpu
from jax.sharding import PartitionSpec as P

WINDOW = 6


LOGIT_SCALE = 10.0
LOGIT_BIAS = -3.0
LOSS_SCALE = 256.0
EPSILON = 1e-06


def shifted(value, axis, steps):
    count = lax.axis_size(axis)
    pairs = [(source, (source + steps) % count) for source in range(count)]
    return lax.ppermute(value, axis, pairs)


def unit_rows(values):
    values = values.astype(jnp.float32)
    inverse = lax.rsqrt(jnp.sum(values * values, axis=-1, keepdims=True) + EPSILON)
    return (values * inverse, inverse)


def pair_grad(images, texts, step_ids, col_ids, position):
    logits = (
        LOGIT_SCALE * jnp.einsum("ie,ke->ik", images, texts, preferred_element_type=jnp.float32)
        + LOGIT_BIAS
    )
    columns = lax.broadcasted_iota(jnp.int32, logits.shape, 1)
    positive = (step_ids[:, None] == position) & (col_ids[:, None] == columns)
    target = jnp.where(positive, 1.0, -1.0).astype(jnp.float32)
    return (-LOSS_SCALE * LOGIT_SCALE * target * jax.nn.sigmoid(-target * logits)).astype(
        jnp.bfloat16
    )


def shard_rows(table, shard, cycle_size, row_count):
    start = (shard + cycle_size) % cycle_size * row_count
    return lax.dynamic_slice_in_dim(table, start, row_count)


def move_block(travel, hop):
    return shifted(travel, "dp", hop)


def local(image_embeds, text_features, projection, pair_step, pair_col):
    cycle_size = lax.axis_size("dp")
    my_index = lax.axis_index("dp")
    row_count = image_embeds.shape[1]
    window_len = min(WINDOW, cycle_size)
    back_reach = window_len // 2 - 1
    unit_img = unit_rows(image_embeds[0])[0].astype(jnp.bfloat16)
    features = text_features[0]
    hidden = jnp.dot(features, projection, preferred_element_type=jnp.float32)
    unit_text, inverse_norm = unit_rows(hidden)
    text_units = unit_text.astype(jnp.bfloat16)
    all_steps = pair_step[0]
    all_cols = pair_col[0]
    streams = [(-back_reach, 0)] + [(1, position) for position in range(1, window_len)]
    my_steps = shard_rows(all_steps, my_index, cycle_size, row_count)
    my_cols = shard_rows(all_cols, my_index, cycle_size, row_count)
    travel = text_units
    running = None
    for hop, position in streams:
        travel = move_block(travel, hop)
        if running is not None:
            running = shifted(running.astype(jnp.bfloat16), "dp", hop).astype(running.dtype)
        weights = pair_grad(unit_img, travel, my_steps, my_cols, position)
        contribution = jnp.einsum(
            "ik,ie->ke", weights, unit_img, preferred_element_type=jnp.float32
        )
        running = contribution if running is None else running + contribution
    unit_grad = shifted(running.astype(jnp.bfloat16), "dp", back_reach - streams[-1][1]).astype(
        running.dtype
    )
    radial = jnp.sum(unit_text * unit_grad, axis=-1, keepdims=True)
    hidden_grad = (inverse_norm * (unit_grad - unit_text * radial)).astype(jnp.bfloat16)
    grad_text = jnp.einsum(
        "ke,de->kd", hidden_grad, projection, preferred_element_type=jnp.float32
    ).astype(jnp.bfloat16)
    partial_value = jnp.einsum(
        "kd,ke->de", features, hidden_grad, preferred_element_type=jnp.float32
    )
    partial_value = lax.optimization_barrier(partial_value.astype(jnp.bfloat16)).astype(jnp.float32)
    pooled = lax.psum_scatter(
        partial_value.astype(jnp.bfloat16), "outer", scatter_dimension=1, tiled=True
    ).astype(jnp.float32)
    owned = lax.psum_scatter(pooled, "dp", scatter_dimension=0, tiled=True)
    global_sq = lax.psum(jnp.sum(owned * owned), ("dp", "outer"))
    threshold = math.sqrt(projection.shape[0] * projection.shape[1])
    factor = jnp.minimum(1.0, threshold / jnp.sqrt(global_sq))
    return (grad_text[None], owned * factor)


CHUNKS = 2
SLAB_LANES = 384
Z_SIZE = 4
QUAD = 4


def rows_ds(start, count):
    return pl.ds(pl.multiple_of(start, 16), count)


def kernel(
    image_ref, text_ref, proj_ref, step_ref, col_ref,
    grad_text_ref, grad_proj_ref,
    img, ftq, hs, hq, unit_text, inv_norm, units, ugrad, hgrad,
    psend, prec, own_part, zsend, zrec, sq_src, sq_quad, sq_mid, sq_dp,
    up_sem, down_sem, side_sem, img_recv, ft_send, ft_recv, h_send, h_recv,
    p_send, p_recv, z_send, z_recv, q_send, q_recv, d_send, d_recv,
):
    bf16, f32 = jnp.bfloat16, jnp.float32
    me = lax.axis_index("dp")
    quad = lax.axis_index("outer")
    n_dp = 2 * Z_SIZE
    z, x = me // 2, me % 2
    rows, width = image_ref.shape
    chunk = rows // CHUNKS
    own_rows, own_cols = grad_proj_ref.shape

    def device(dp, outer):
        return {"dp": dp, "outer": outer}

    barrier = pltpu.get_barrier_semaphore()
    for i in range(1, QUAD):
        pl.semaphore_signal(barrier, inc=1, device_id=device(me, (quad + i) % QUAD),
                            device_id_type=pl.DeviceIdType.MESH)
    for i in range(1, n_dp):
        pl.semaphore_signal(barrier, inc=1, device_id=device((me + i) % n_dp, quad),
                            device_id_type=pl.DeviceIdType.MESH)

    values = image_ref[...].astype(f32)
    inverse = lax.rsqrt(jnp.sum(values * values, axis=-1, keepdims=True) + EPSILON)
    img[me] = (values * inverse).astype(bf16)
    pl.semaphore_wait(barrier, QUAD - 1 + n_dp - 1)

    def image_copy(block, part, target, send_sem):
        where = img.at[block, pl.ds(part * chunk, chunk)]
        return pltpu.make_async_remote_copy(
            src_ref=where, dst_ref=where, send_sem=send_sem, recv_sem=img_recv.at[block, part],
            device_id=device(target, quad), device_id_type=pl.DeviceIdType.MESH)

    def up(zs, part):
        return image_copy(2 * zs + x, part, me + 2, up_sem.at[zs, part])

    def down(zs, part):
        return image_copy(2 * zs + x, part, me - 2, down_sem.at[zs, part])

    def side(zs, part):
        return image_copy(2 * zs + x, part, me + 1 - 2 * x, side_sem.at[zs, part])

    def arrived(block, part):
        image_copy(block, part, me, side_sem.at[0, part]).wait_recv()

    def wanted(at, zs):
        return jnp.logical_or(x == 0, (zs + 2) % Z_SIZE != at)

    def reaches(at, zs):
        inner = jnp.logical_and(at > 0, at < Z_SIZE - 1)
        return jnp.logical_or(inner, wanted(at, zs))

    def goes_side(zs):
        ahead = (zs - z + Z_SIZE) % Z_SIZE
        return jnp.logical_or(ahead == 1, ahead == 2 + x)

    def relayed(distance, act):
        for part in range(CHUNKS):
            for sign in (1, -1):
                zs = z + sign * distance
                inside = zs < Z_SIZE if sign == 1 else zs >= 0
                here = jnp.logical_and(inside, reaches(z, zs))
                beyond = z - sign
                further = beyond >= 0 if sign == 1 else beyond < Z_SIZE
                act(zs, part, here,
                    jnp.logical_and(jnp.logical_and(inside, further), reaches(beyond, zs)),
                    jnp.logical_and(here, goes_side(zs)),
                    down if sign == 1 else up)

    def relay(distance):
        def act(zs, part, here, onward, aside, onward_copy):
            @pl.when(here)
            def _():
                arrived(2 * zs + x, part)

                @pl.when(onward)
                def _():
                    onward_copy(zs, part).start()

                @pl.when(aside)
                def _():
                    side(zs, part).start()

        relayed(distance, act)

    def finish_relay(distance):
        def act(zs, part, here, onward, aside, onward_copy):
            @pl.when(onward)
            def _():
                onward_copy(zs, part).wait_send()

            @pl.when(aside)
            def _():
                side(zs, part).wait_send()

        relayed(distance, act)

    for part in range(CHUNKS):
        @pl.when(z < Z_SIZE - 1)
        def _():
            up(z, part).start()

        @pl.when(z > 0)
        def _():
            down(z, part).start()

        side(z, part).start()

    turned = text_ref[...].astype(f32).T
    for zc in range(Z_SIZE):
        for xc in range(2):
            at = (2 * zc + xc) * own_rows
            ftq[quad, pl.ds((xc * Z_SIZE + zc) * own_rows, own_rows)] = (
                turned[at:at + own_rows].astype(bf16))

    def ft_copy(source, i):
        return pltpu.make_async_remote_copy(
            src_ref=ftq.at[source], dst_ref=ftq.at[source], send_sem=ft_send.at[i],
            recv_sem=ft_recv.at[source], device_id=device(me, (quad + i) % QUAD),
            device_id_type=pl.DeviceIdType.MESH)

    for i in range(1, QUAD):
        ft_copy(quad, i).start()

    hidden = jnp.dot(text_ref[...], proj_ref[...], preferred_element_type=f32)
    inv = lax.rsqrt(jnp.sum(hidden * hidden, axis=-1, keepdims=True) + EPSILON)
    inv_norm[...] = jnp.broadcast_to(inv, inv_norm.shape)
    unit = hidden * inv
    unit_text[...] = unit
    units[...] = unit.astype(bf16)

    def pair_step(block, first=False):
        if not first:
            for part in range(CHUNKS):
                @pl.when(needs_wait(block))
                def _():
                    arrived(block, part)
        position = (block - me + 2 + n_dp) % n_dp
        images = img[block]
        dots = lax.dot_general(units[...], images, (((1,), (1,)), ((), ())),
                               preferred_element_type=f32)
        logits = LOGIT_SCALE * dots + LOGIT_BIAS
        columns = lax.broadcasted_iota(jnp.int32, logits.shape, 0)
        positive = jnp.logical_and(step_ref[pl.ds(block, 1), :] == position,
                                   col_ref[pl.ds(block, 1), :] == columns)
        target = jnp.where(positive, 1.0, -1.0).astype(f32)
        weights = (-LOSS_SCALE * LOGIT_SCALE * target * jax.nn.sigmoid(-target * logits)).astype(bf16)
        term = jnp.dot(weights, images, preferred_element_type=f32)
        if first:
            ugrad[...] = term
        else:
            ugrad[...] += term

    def needs_wait(block):
        return block % 2 != x

    ahead, behind = (z + 1) % Z_SIZE, (z + Z_SIZE - 1) % Z_SIZE
    third = jnp.where(x == 0, behind, (z + 2) % Z_SIZE)
    col_ahead, col_behind = 2 * ahead + x, 2 * behind + x
    side_ahead, side_third = 2 * ahead + 1 - x, 2 * third + 1 - x
    low, high = z == 0, z == Z_SIZE - 1
    order = (
        2 * z + 1 - x,
        jnp.where(high, col_behind, col_ahead),
        jnp.where(low, side_ahead, jnp.where(high, side_third, col_behind)),
        jnp.where(low, side_third, jnp.where(high, col_ahead, side_ahead)),
        jnp.where(low, col_behind, jnp.where(high, side_ahead, side_third)),
    )
    pair_step(me, first=True)
    relay(1)
    pair_step(order[0])
    pair_step(order[1])
    relay(2)
    pair_step(order[2])
    relay(3)
    pair_step(order[3])
    pair_step(order[4])

    unit = unit_text[...]
    total = ugrad[...]
    radial = jnp.sum(unit * total, axis=-1, keepdims=True)
    hidden_grad = (inv_norm[:, :1] * (total - unit * radial)).astype(bf16)
    hgrad[...] = hidden_grad
    wide = hidden_grad.astype(f32)
    for c in range(QUAD):
        moved = wide if c == 0 else pltpu.roll(wide, width - c * own_cols, 1)
        hs[c] = moved[:, :SLAB_LANES].astype(bf16)

    def h_copy(source, i):
        return pltpu.make_async_remote_copy(
            src_ref=hs.at[(quad + i) % QUAD], dst_ref=hq.at[source], send_sem=h_send.at[i],
            recv_sem=h_recv.at[source], device_id=device(me, (quad + i) % QUAD),
            device_id_type=pl.DeviceIdType.MESH)

    for i in range(1, QUAD):
        h_copy(quad, i).start()
    hq[quad] = hs[quad]
    grad_text_ref[...] = lax.dot_general(
        hgrad[...], proj_ref[...], (((1,), (1,)), ((), ())), preferred_element_type=f32
    ).astype(bf16)

    for i in range(1, QUAD):
        source = (quad + i) % QUAD
        ft_copy(source, i).wait_recv()
        h_copy(source, i).wait_recv()

    half = Z_SIZE * own_rows

    def half_sum(which):
        acc = None
        for q in range(QUAD):
            term = jnp.dot(ftq[q, rows_ds(which * half, half)], hq[q], preferred_element_type=f32)
            acc = term if acc is None else acc + term
        return acc

    def p_copy(zc):
        return pltpu.make_async_remote_copy(
            src_ref=psend.at[zc], dst_ref=prec.at[zc], send_sem=p_send.at[zc],
            recv_sem=p_recv.at[zc], device_id=device(me + 1 - 2 * x, quad),
            device_id_type=pl.DeviceIdType.MESH)

    part_sum = half_sum(1 - x)
    for zc in range(Z_SIZE):
        psend[zc] = part_sum[zc * own_rows:(zc + 1) * own_rows].astype(bf16)
        p_copy(zc).start()
    part_sum = half_sum(x)
    for zc in range(Z_SIZE):
        own_part[zc] = part_sum[zc * own_rows:(zc + 1) * own_rows]

    def z_copy(source, i):
        return pltpu.make_async_remote_copy(
            src_ref=zsend.at[i], dst_ref=zrec.at[source], send_sem=z_send.at[i],
            recv_sem=z_recv.at[source], device_id=device((me + 2 * i) % n_dp, quad),
            device_id_type=pl.DeviceIdType.MESH)

    for i in range(1, Z_SIZE):
        to = (z + i) % Z_SIZE
        p_copy(to).wait_recv()
        zsend[i] = (own_part[to] + prec[to].astype(f32)).astype(bf16)
        z_copy(z, i).start()
    p_copy(z).wait_recv()
    owned = own_part[z] + prec[z].astype(f32)
    for i in range(1, Z_SIZE):
        source = (z + i) % Z_SIZE
        z_copy(source, i).wait_recv()
        owned = owned + zrec[source].astype(f32)

    lanes = lax.broadcasted_iota(jnp.int32, owned.shape, 1)
    kept = jnp.where(lanes < own_cols, owned, 0.0)
    mine = jnp.sum(kept * kept)
    sq_src[...] = jnp.broadcast_to(mine, sq_src.shape)

    def q_copy(source, i):
        return pltpu.make_async_remote_copy(
            src_ref=sq_src, dst_ref=sq_quad.at[source], send_sem=q_send.at[i],
            recv_sem=q_recv.at[source], device_id=device(me, (quad + i) % QUAD),
            device_id_type=pl.DeviceIdType.MESH)

    def d_copy(source, i):
        return pltpu.make_async_remote_copy(
            src_ref=sq_mid, dst_ref=sq_dp.at[source], send_sem=d_send.at[i],
            recv_sem=d_recv.at[source], device_id=device((me + i) % n_dp, quad),
            device_id_type=pl.DeviceIdType.MESH)

    for i in range(1, QUAD):
        q_copy(quad, i).start()
    sq_quad[quad] = sq_src[...]
    for i in range(1, QUAD):
        q_copy((quad + i) % QUAD, i).wait_recv()
    sq_mid[...] = sq_quad[0] + sq_quad[1] + sq_quad[2] + sq_quad[3]
    for i in range(1, n_dp):
        d_copy(me, i).start()
    sq_dp[me] = sq_mid[...]

    for part in range(CHUNKS):
        @pl.when(z < Z_SIZE - 1)
        def _():
            up(z, part).wait_send()

        @pl.when(z > 0)
        def _():
            down(z, part).wait_send()

        side(z, part).wait_send()
    for distance in range(1, Z_SIZE):
        finish_relay(distance)
    for i in range(1, QUAD):
        ft_copy(quad, i).wait_send()
        h_copy(quad, i).wait_send()
        q_copy(quad, i).wait_send()
    for zc in range(Z_SIZE):
        p_copy(zc).wait_send()
    for i in range(1, Z_SIZE):
        z_copy(z, i).wait_send()

    for i in range(1, n_dp):
        d_copy((me + i) % n_dp, i).wait_recv()
    global_sq = sq_dp[0]
    for i in range(1, n_dp):
        global_sq = global_sq + sq_dp[i]
    threshold = math.sqrt(width * proj_ref.shape[0])
    factor = jnp.minimum(1.0, threshold / jnp.sqrt(global_sq[:1, :1]))
    grad_proj_ref[...] = owned[:, :own_cols] * factor
    for i in range(1, n_dp):
        d_copy(me, i).wait_send()


def fused(image_embeds, text_features, projection, pair_step, pair_col):
    n_dp, n_outer = lax.axis_size("dp"), lax.axis_size("outer")
    rows, width = image_embeds.shape[1:]
    depth = projection.shape[0]
    own_rows, own_cols = depth // n_dp, width // n_outer
    bf16, f32 = jnp.bfloat16, jnp.float32
    dma = pltpu.SemaphoreType.DMA
    vmem = pl.BlockSpec(memory_space=pltpu.VMEM)
    slab = (own_rows, SLAB_LANES)
    grad_text, grad_proj = pl.pallas_call(
        kernel,
        out_shape=(
            jax.ShapeDtypeStruct((rows, depth), bf16),
            jax.ShapeDtypeStruct((own_rows, own_cols), f32),
        ),
        in_specs=[vmem] * 5,
        out_specs=(vmem, vmem),
        scratch_shapes=[
            pltpu.VMEM((n_dp, rows, width), bf16),
            pltpu.VMEM((QUAD, depth, rows), bf16),
            pltpu.VMEM((QUAD, rows, SLAB_LANES), bf16),
            pltpu.VMEM((QUAD, rows, SLAB_LANES), bf16),
            pltpu.VMEM((rows, width), f32),
            pltpu.VMEM((rows, 128), f32),
            pltpu.VMEM((rows, width), bf16),
            pltpu.VMEM((rows, width), f32),
            pltpu.VMEM((rows, width), bf16),
            pltpu.VMEM((Z_SIZE, *slab), bf16),
            pltpu.VMEM((Z_SIZE, *slab), bf16),
            pltpu.VMEM((Z_SIZE, *slab), f32),
            pltpu.VMEM((Z_SIZE, *slab), bf16),
            pltpu.VMEM((Z_SIZE, *slab), bf16),
            pltpu.VMEM((8, 128), f32),
            pltpu.VMEM((QUAD, 8, 128), f32),
            pltpu.VMEM((8, 128), f32),
            pltpu.VMEM((n_dp, 8, 128), f32),
            dma((Z_SIZE, CHUNKS)), dma((Z_SIZE, CHUNKS)), dma((Z_SIZE, CHUNKS)),
            dma((n_dp, CHUNKS)),
            dma((QUAD,)), dma((QUAD,)), dma((QUAD,)), dma((QUAD,)),
            dma((Z_SIZE,)), dma((Z_SIZE,)), dma((Z_SIZE,)), dma((Z_SIZE,)),
            dma((QUAD,)), dma((QUAD,)), dma((n_dp,)), dma((n_dp,)),
        ],
        compiler_params=pltpu.CompilerParams(
            collective_id=0, has_side_effects=True, vmem_limit_bytes=48 * 1024 * 1024
        ),
        cost_estimate=pl.CostEstimate(
            flops=2 * rows * depth * width * 3 + 4 * WINDOW * rows * rows * width,
            bytes_accessed=2 * (4 * rows * width + depth * width),
            transcendentals=WINDOW * rows * rows,
        ),
    )(
        image_embeds[0], text_features[0], projection,
        pair_step.reshape(n_dp, rows), pair_col.reshape(n_dp, rows),
    )
    return grad_text[None], grad_proj


def solution(mesh):
    placed = (
        P("outer", "dp", None),
        P("outer", "dp", None),
        P(),
        P("outer", None),
        P("outer", None),
    )
    small = mesh.shape["dp"] == 2 * Z_SIZE and mesh.shape["outer"] == QUAD
    return jax.shard_map(
        fused if small else local,
        mesh=mesh,
        in_specs=placed,
        out_specs=(P("outer", "dp", None), P("dp", "outer")),
        check_vma=False,
    )
```

```python
import math

import jax
import jax.numpy as jnp
from jax import lax
from jax.experimental import pallas as pl
from jax.experimental.pallas import tpu as pltpu
from jax.sharding import PartitionSpec as P

WINDOW = 6


LOGIT_SCALE = 10.0
LOGIT_BIAS = -3.0
LOSS_SCALE = 256.0
EPSILON = 1e-06


def shifted(value, axis, steps):
    count = lax.axis_size(axis)
    pairs = [(source, (source + steps) % count) for source in range(count)]
    return lax.ppermute(value, axis, pairs)


def unit_rows(values):
    values = values.astype(jnp.float32)
    inverse = lax.rsqrt(jnp.sum(values * values, axis=-1, keepdims=True) + EPSILON)
    return (values * inverse, inverse)


def pair_grad(images, texts, step_ids, col_ids, position):
    logits = (
        LOGIT_SCALE * jnp.einsum("ie,ke->ik", images, texts, preferred_element_type=jnp.float32)
        + LOGIT_BIAS
    )
    columns = lax.broadcasted_iota(jnp.int32, logits.shape, 1)
    positive = (step_ids[:, None] == position) & (col_ids[:, None] == columns)
    target = jnp.where(positive, 1.0, -1.0).astype(jnp.float32)
    return (-LOSS_SCALE * LOGIT_SCALE * target * jax.nn.sigmoid(-target * logits)).astype(
        jnp.bfloat16
    )


def shard_rows(table, shard, cycle_size, row_count):
    start = (shard + cycle_size) % cycle_size * row_count
    return lax.dynamic_slice_in_dim(table, start, row_count)


def move_block(travel, hop):
    return shifted(travel, "dp", hop)


def local(image_embeds, text_features, projection, pair_step, pair_col):
    cycle_size = lax.axis_size("dp")
    my_index = lax.axis_index("dp")
    row_count = image_embeds.shape[1]
    window_len = min(WINDOW, cycle_size)
    back_reach = window_len // 2 - 1
    unit_img = unit_rows(image_embeds[0])[0].astype(jnp.bfloat16)
    features = text_features[0]
    hidden = jnp.dot(features, projection, preferred_element_type=jnp.float32)
    unit_text, inverse_norm = unit_rows(hidden)
    text_units = unit_text.astype(jnp.bfloat16)
    all_steps = pair_step[0]
    all_cols = pair_col[0]
    streams = [(-back_reach, 0)] + [(1, position) for position in range(1, window_len)]
    my_steps = shard_rows(all_steps, my_index, cycle_size, row_count)
    my_cols = shard_rows(all_cols, my_index, cycle_size, row_count)
    travel = text_units
    running = None
    for hop, position in streams:
        travel = move_block(travel, hop)
        if running is not None:
            running = shifted(running.astype(jnp.bfloat16), "dp", hop).astype(running.dtype)
        weights = pair_grad(unit_img, travel, my_steps, my_cols, position)
        contribution = jnp.einsum(
            "ik,ie->ke", weights, unit_img, preferred_element_type=jnp.float32
        )
        running = contribution if running is None else running + contribution
    unit_grad = shifted(running.astype(jnp.bfloat16), "dp", back_reach - streams[-1][1]).astype(
        running.dtype
    )
    radial = jnp.sum(unit_text * unit_grad, axis=-1, keepdims=True)
    hidden_grad = (inverse_norm * (unit_grad - unit_text * radial)).astype(jnp.bfloat16)
    grad_text = jnp.einsum(
        "ke,de->kd", hidden_grad, projection, preferred_element_type=jnp.float32
    ).astype(jnp.bfloat16)
    partial_value = jnp.einsum(
        "kd,ke->de", features, hidden_grad, preferred_element_type=jnp.float32
    )
    partial_value = lax.optimization_barrier(partial_value.astype(jnp.bfloat16)).astype(jnp.float32)
    pooled = lax.psum_scatter(
        partial_value.astype(jnp.bfloat16), "outer", scatter_dimension=1, tiled=True
    ).astype(jnp.float32)
    owned = lax.psum_scatter(pooled, "dp", scatter_dimension=0, tiled=True)
    global_sq = lax.psum(jnp.sum(owned * owned), ("dp", "outer"))
    threshold = math.sqrt(projection.shape[0] * projection.shape[1])
    factor = jnp.minimum(1.0, threshold / jnp.sqrt(global_sq))
    return (grad_text[None], owned * factor)


CHUNKS = 2
LANES = 128
Z_SIZE = 4
QUAD = 4


def rows_ds(start, count):
    return pl.ds(pl.multiple_of(start, 16), count)


def kernel(
    image_hbm, text_hbm, proj_hbm, step_hbm, col_hbm,
    grad_text_ref, grad_proj_ref,
    image_ref, text_ref, proj_ref, step_ref, col_ref, load_sem,
    img, ftq, hs, hq, unit_text, inv_norm, units, ugrad, hgrad,
    psend, prec, own_part, zsend, zrec, sq_src, sq_quad, sq_mid, sq_dp,
    up_sem, down_sem, side_sem, img_recv, ft_send, ft_recv, h_send, h_recv,
    p_send, p_recv, z_send, z_recv, q_send, q_recv, d_send, d_recv,
):
    bf16, f32 = jnp.bfloat16, jnp.float32
    me = lax.axis_index("dp")
    quad = lax.axis_index("outer")
    n_dp = 2 * Z_SIZE
    z, x = me // 2, me % 2
    rows, width = image_ref.shape
    chunk = rows // CHUNKS
    own_rows, own_cols = grad_proj_ref.shape

    def device(dp, outer):
        return {"dp": dp, "outer": outer}

    loads = [
        pltpu.make_async_copy(source, target, load_sem.at[i])
        for i, (source, target) in enumerate((
            (image_hbm.at[0], image_ref), (text_hbm.at[0], text_ref), (proj_hbm, proj_ref),
            (step_hbm, step_ref), (col_hbm, col_ref)))
    ]
    for load in loads:
        load.start()

    barrier = pltpu.get_barrier_semaphore()
    for i in range(1, QUAD):
        pl.semaphore_signal(barrier, inc=1, device_id=device(me, (quad + i) % QUAD),
                            device_id_type=pl.DeviceIdType.MESH)
    for i in range(1, n_dp):
        pl.semaphore_signal(barrier, inc=1, device_id=device((me + i) % n_dp, quad),
                            device_id_type=pl.DeviceIdType.MESH)

    loads[0].wait()
    values = image_ref[...].astype(f32)
    inverse = lax.rsqrt(jnp.sum(values * values, axis=-1, keepdims=True) + EPSILON)
    img[me] = (values * inverse).astype(bf16)
    pl.semaphore_wait(barrier, QUAD - 1 + n_dp - 1)

    def image_copy(block, part, target, send_sem):
        where = img.at[block, pl.ds(part * chunk, chunk)]
        return pltpu.make_async_remote_copy(
            src_ref=where, dst_ref=where, send_sem=send_sem, recv_sem=img_recv.at[block, part],
            device_id=device(target, quad), device_id_type=pl.DeviceIdType.MESH)

    def up(zs, part):
        return image_copy(2 * zs + x, part, me + 2, up_sem.at[zs, part])

    def down(zs, part):
        return image_copy(2 * zs + x, part, me - 2, down_sem.at[zs, part])

    def side(zs, part):
        return image_copy(2 * zs + x, part, me + 1 - 2 * x, side_sem.at[zs, part])

    def arrived(block, part):
        image_copy(block, part, me, side_sem.at[0, part]).wait_recv()

    def wanted(at, zs):
        return jnp.logical_or(x == 0, (zs + 2) % Z_SIZE != at)

    def reaches(at, zs):
        inner = jnp.logical_and(at > 0, at < Z_SIZE - 1)
        return jnp.logical_or(inner, wanted(at, zs))

    def goes_side(zs):
        ahead = (zs - z + Z_SIZE) % Z_SIZE
        return jnp.logical_or(ahead == 1, ahead == 2 + x)

    def relayed(distance, act, parts=range(CHUNKS)):
        for part in parts:
            for sign in (1, -1):
                zs = z + sign * distance
                inside = zs < Z_SIZE if sign == 1 else zs >= 0
                here = jnp.logical_and(inside, reaches(z, zs))
                beyond = z - sign
                further = beyond >= 0 if sign == 1 else beyond < Z_SIZE
                act(zs, part, here,
                    jnp.logical_and(jnp.logical_and(inside, further), reaches(beyond, zs)),
                    jnp.logical_and(here, goes_side(zs)),
                    down if sign == 1 else up)

    def relay(distance, parts=range(CHUNKS)):
        def act(zs, part, here, onward, aside, onward_copy):
            @pl.when(here)
            def _():
                arrived(2 * zs + x, part)

                @pl.when(onward)
                def _():
                    onward_copy(zs, part).start()

                @pl.when(aside)
                def _():
                    side(zs, part).start()

        relayed(distance, act, parts)

    def finish_relay(distance):
        def act(zs, part, here, onward, aside, onward_copy):
            @pl.when(onward)
            def _():
                onward_copy(zs, part).wait_send()

            @pl.when(aside)
            def _():
                side(zs, part).wait_send()

        relayed(distance, act)

    for part in range(CHUNKS):
        @pl.when(z < Z_SIZE - 1)
        def _():
            up(z, part).start()

        @pl.when(z > 0)
        def _():
            down(z, part).start()

        side(z, part).start()

    loads[1].wait()
    turned = text_ref[...].astype(f32).T
    for zc in range(Z_SIZE):
        for xc in range(2):
            at = (2 * zc + xc) * own_rows
            ftq[quad, pl.ds((xc * Z_SIZE + zc) * own_rows, own_rows)] = (
                turned[at:at + own_rows].astype(bf16))

    def ft_copy(source, i):
        return pltpu.make_async_remote_copy(
            src_ref=ftq.at[source], dst_ref=ftq.at[source], send_sem=ft_send.at[i],
            recv_sem=ft_recv.at[source], device_id=device(me, (quad + i) % QUAD),
            device_id_type=pl.DeviceIdType.MESH)

    for i in range(1, QUAD):
        ft_copy(quad, i).start()

    loads[2].wait()
    hidden = jnp.dot(text_ref[...], proj_ref[...], preferred_element_type=f32)
    inv = lax.rsqrt(jnp.sum(hidden * hidden, axis=-1, keepdims=True) + EPSILON)
    inv_norm[...] = jnp.broadcast_to(inv, inv_norm.shape)
    unit = hidden * inv
    unit_text[...] = unit
    units[...] = unit.astype(bf16)
    loads[3].wait()
    loads[4].wait()

    def pair_step(block, parts, first=False):
        if not first:
            for part in parts:
                @pl.when(needs_wait(block))
                def _():
                    arrived(block, part)
        position = (block - me + 2 + n_dp) % n_dp
        start, count = parts[0] * chunk, len(parts) * chunk
        images = img[block, pl.ds(start, count)]
        dots = lax.dot_general(units[...], images, (((1,), (1,)), ((), ())),
                               preferred_element_type=f32)
        logits = LOGIT_SCALE * dots + LOGIT_BIAS
        columns = lax.broadcasted_iota(jnp.int32, logits.shape, 0)
        where = pl.ds(pl.multiple_of(block * rows + start, LANES), count)
        positive = jnp.logical_and(step_ref[:, where] == position, col_ref[:, where] == columns)
        target = jnp.where(positive, 1.0, -1.0).astype(f32)
        weights = (-LOSS_SCALE * LOGIT_SCALE * target * jax.nn.sigmoid(-target * logits)).astype(bf16)
        term = jnp.dot(weights, images, preferred_element_type=f32)
        if first:
            ugrad[...] = term
        else:
            ugrad[...] += term

    def needs_wait(block):
        return block % 2 != x

    ahead, behind = (z + 1) % Z_SIZE, (z + Z_SIZE - 1) % Z_SIZE
    third = jnp.where(x == 0, behind, (z + 2) % Z_SIZE)
    col_ahead, col_behind = 2 * ahead + x, 2 * behind + x
    side_ahead, side_third = 2 * ahead + 1 - x, 2 * third + 1 - x
    low, high = z == 0, z == Z_SIZE - 1
    order = (
        2 * z + 1 - x,
        jnp.where(high, col_behind, col_ahead),
        jnp.where(low, side_ahead, jnp.where(high, side_third, col_behind)),
        jnp.where(low, side_third, jnp.where(high, col_ahead, side_ahead)),
        jnp.where(low, col_behind, jnp.where(high, side_ahead, side_third)),
    )
    every = range(CHUNKS)
    pair_step(me, every, first=True)
    relay(1)
    pair_step(order[0], every)
    pair_step(order[1], every)
    relay(2)
    pair_step(order[2], every)
    for part in every:
        relay(3, (part,))
        pair_step(order[3], (part,))
        pair_step(order[4], (part,))

    unit = unit_text[...]
    total = ugrad[...]
    radial = jnp.sum(unit * total, axis=-1, keepdims=True)
    hidden_grad = (inv_norm[:, :1] * (total - unit * radial)).astype(bf16)
    hgrad[...] = hidden_grad
    wide = hidden_grad.astype(f32)
    slices = -(-own_cols // LANES)
    for c in range(QUAD):
        moved = wide if c == 0 else pltpu.roll(wide, width - c * own_cols, 1)
        for s in range(slices):
            hs[c, s] = moved[:, s * LANES:(s + 1) * LANES].astype(bf16)

    def h_copy(source, i, s):
        return pltpu.make_async_remote_copy(
            src_ref=hs.at[(quad + i) % QUAD, s], dst_ref=hq.at[source, s],
            send_sem=h_send.at[i, s], recv_sem=h_recv.at[source, s],
            device_id=device(me, (quad + i) % QUAD), device_id_type=pl.DeviceIdType.MESH)

    for s in range(slices):
        for i in range(1, QUAD):
            h_copy(quad, i, s).start()
    hq[quad] = hs[quad]
    grad_text_ref[0] = lax.dot_general(
        hgrad[...], proj_ref[...], (((1,), (1,)), ((), ())), preferred_element_type=f32
    ).astype(bf16)

    for i in range(1, QUAD):
        ft_copy((quad + i) % QUAD, i).wait_recv()

    half = Z_SIZE * own_rows

    def half_sum(which, s):
        acc = None
        for q in range(QUAD):
            term = jnp.dot(ftq[q, rows_ds(which * half, half)], hq[q, s],
                           preferred_element_type=f32)
            acc = term if acc is None else acc + term
        return acc

    def p_copy(zc, s):
        return pltpu.make_async_remote_copy(
            src_ref=psend.at[s, zc], dst_ref=prec.at[s, zc], send_sem=p_send.at[zc, s],
            recv_sem=p_recv.at[zc, s], device_id=device(me + 1 - 2 * x, quad),
            device_id_type=pl.DeviceIdType.MESH)

    def z_copy(source, i, s):
        return pltpu.make_async_remote_copy(
            src_ref=zsend.at[s, i], dst_ref=zrec.at[s, source], send_sem=z_send.at[i, s],
            recv_sem=z_recv.at[source, s], device_id=device((me + 2 * i) % n_dp, quad),
            device_id_type=pl.DeviceIdType.MESH)

    def send_half(s):
        for i in range(1, QUAD):
            h_copy((quad + i) % QUAD, i, s).wait_recv()
        part_sum = half_sum(1 - x, s)
        for zc in range(Z_SIZE):
            psend[s, zc] = part_sum[zc * own_rows:(zc + 1) * own_rows].astype(bf16)
            p_copy(zc, s).start()
        part_sum = half_sum(x, s)
        for zc in range(Z_SIZE):
            own_part[s, zc] = part_sum[zc * own_rows:(zc + 1) * own_rows]

    def send_owners(s):
        for i in (2, 1, 3):
            to = (z + i) % Z_SIZE
            p_copy(to, s).wait_recv()
            zsend[s, i] = (own_part[s, to] + prec[s, to].astype(f32)).astype(bf16)
            z_copy(z, i, s).start()

    def finished(s):
        p_copy(z, s).wait_recv()
        owned = own_part[s, z] + prec[s, z].astype(f32)
        for i in range(1, Z_SIZE):
            source = (z + i) % Z_SIZE
            z_copy(source, i, s).wait_recv()
            owned = owned + zrec[s, source].astype(f32)
        lanes = lax.broadcasted_iota(jnp.int32, owned.shape, 1)
        return jnp.where(lanes < own_cols - s * LANES, owned, 0.0)

    for s in range(slices):
        send_half(s)
        if s > 0:
            send_owners(s - 1)
    send_owners(slices - 1)
    owned = [finished(s) for s in range(slices)]
    squares = owned[0] * owned[0]
    for piece in owned[1:]:
        squares = squares + piece * piece
    sq_src[...] = jnp.broadcast_to(jnp.sum(squares), sq_src.shape)

    def q_copy(source, i):
        return pltpu.make_async_remote_copy(
            src_ref=sq_src, dst_ref=sq_quad.at[source], send_sem=q_send.at[i],
            recv_sem=q_recv.at[source], device_id=device(me, (quad + i) % QUAD),
            device_id_type=pl.DeviceIdType.MESH)

    def d_copy(source, i):
        return pltpu.make_async_remote_copy(
            src_ref=sq_mid, dst_ref=sq_dp.at[source], send_sem=d_send.at[i],
            recv_sem=d_recv.at[source], device_id=device((me + i) % n_dp, quad),
            device_id_type=pl.DeviceIdType.MESH)

    for i in range(1, QUAD):
        q_copy(quad, i).start()
    sq_quad[quad] = sq_src[...]
    for i in range(1, QUAD):
        q_copy((quad + i) % QUAD, i).wait_recv()
    sq_mid[...] = sq_quad[0] + sq_quad[1] + sq_quad[2] + sq_quad[3]
    for i in range(1, n_dp):
        d_copy(me, i).start()
    sq_dp[me] = sq_mid[...]

    for part in range(CHUNKS):
        @pl.when(z < Z_SIZE - 1)
        def _():
            up(z, part).wait_send()

        @pl.when(z > 0)
        def _():
            down(z, part).wait_send()

        side(z, part).wait_send()
    for distance in range(1, Z_SIZE):
        finish_relay(distance)
    for i in range(1, QUAD):
        ft_copy(quad, i).wait_send()
        for s in range(slices):
            h_copy(quad, i, s).wait_send()
        q_copy(quad, i).wait_send()
    for s in range(slices):
        for zc in range(Z_SIZE):
            p_copy(zc, s).wait_send()
        for i in range(1, Z_SIZE):
            z_copy(z, i, s).wait_send()

    for i in range(1, n_dp):
        d_copy((me + i) % n_dp, i).wait_recv()
    global_sq = sq_dp[0]
    for i in range(1, n_dp):
        global_sq = global_sq + sq_dp[i]
    threshold = math.sqrt(width * proj_ref.shape[0])
    factor = jnp.minimum(1.0, threshold / jnp.sqrt(global_sq[:1, :1]))
    for s in range(slices):
        count = min(LANES, own_cols - s * LANES)
        grad_proj_ref[:, s * LANES:s * LANES + count] = owned[s][:, :count] * factor
    for i in range(1, n_dp):
        d_copy(me, i).wait_send()


def fused(image_embeds, text_features, projection, pair_step, pair_col):
    n_dp, n_outer = lax.axis_size("dp"), lax.axis_size("outer")
    rows, width = image_embeds.shape[1:]
    depth = projection.shape[0]
    own_rows, own_cols = depth // n_dp, width // n_outer
    bf16, f32 = jnp.bfloat16, jnp.float32
    dma = pltpu.SemaphoreType.DMA
    vmem = pl.BlockSpec(memory_space=pltpu.VMEM)
    anywhere = pl.BlockSpec(memory_space=pl.ANY)
    slices = -(-own_cols // LANES)
    slab = (own_rows, LANES)
    grad_text, grad_proj = pl.pallas_call(
        kernel,
        out_shape=(
            jax.ShapeDtypeStruct((1, rows, depth), bf16),
            jax.ShapeDtypeStruct((own_rows, own_cols), f32),
        ),
        in_specs=[anywhere] * 5,
        out_specs=(vmem, vmem),
        scratch_shapes=[
            pltpu.VMEM((rows, width), bf16),
            pltpu.VMEM((rows, depth), bf16),
            pltpu.VMEM((depth, width), bf16),
            pltpu.VMEM((1, n_dp * rows), jnp.int32),
            pltpu.VMEM((1, n_dp * rows), jnp.int32),
            dma((5,)),
            pltpu.VMEM((n_dp, rows, width), bf16),
            pltpu.VMEM((QUAD, depth, rows), bf16),
            pltpu.VMEM((QUAD, slices, rows, LANES), bf16),
            pltpu.VMEM((QUAD, slices, rows, LANES), bf16),
            pltpu.VMEM((rows, width), f32),
            pltpu.VMEM((rows, 128), f32),
            pltpu.VMEM((rows, width), bf16),
            pltpu.VMEM((rows, width), f32),
            pltpu.VMEM((rows, width), bf16),
            pltpu.VMEM((slices, Z_SIZE, *slab), bf16),
            pltpu.VMEM((slices, Z_SIZE, *slab), bf16),
            pltpu.VMEM((slices, Z_SIZE, *slab), f32),
            pltpu.VMEM((slices, Z_SIZE, *slab), bf16),
            pltpu.VMEM((slices, Z_SIZE, *slab), bf16),
            pltpu.VMEM((8, 128), f32),
            pltpu.VMEM((QUAD, 8, 128), f32),
            pltpu.VMEM((8, 128), f32),
            pltpu.VMEM((n_dp, 8, 128), f32),
            dma((Z_SIZE, CHUNKS)), dma((Z_SIZE, CHUNKS)), dma((Z_SIZE, CHUNKS)),
            dma((n_dp, CHUNKS)),
            dma((QUAD,)), dma((QUAD,)), dma((QUAD, slices)), dma((QUAD, slices)),
            dma((Z_SIZE, slices)), dma((Z_SIZE, slices)),
            dma((Z_SIZE, slices)), dma((Z_SIZE, slices)),
            dma((QUAD,)), dma((QUAD,)), dma((n_dp,)), dma((n_dp,)),
        ],
        compiler_params=pltpu.CompilerParams(
            collective_id=0, has_side_effects=True, vmem_limit_bytes=60 * 1024 * 1024
        ),
        cost_estimate=pl.CostEstimate(
            flops=2 * rows * depth * width * 3 + 4 * WINDOW * rows * rows * width,
            bytes_accessed=2 * (4 * rows * width + depth * width),
            transcendentals=WINDOW * rows * rows,
        ),
    )(
        image_embeds, text_features, projection, pair_step, pair_col
    )
    return grad_text, grad_proj


def solution(mesh):
    placed = (
        P("outer", "dp", None),
        P("outer", "dp", None),
        P(),
        P("outer", None),
        P("outer", None),
    )
    small = mesh.shape["dp"] == 2 * Z_SIZE and mesh.shape["outer"] == QUAD
    return jax.shard_map(
        fused if small else local,
        mesh=mesh,
        in_specs=placed,
        out_specs=(P("outer", "dp", None), P("dp", "outer")),
        check_vma=False,
    )
```

```python
import math

import jax
import jax.numpy as jnp
from jax import lax
from jax.experimental import pallas as pl
from jax.experimental.pallas import tpu as pltpu
from jax.sharding import PartitionSpec as P

WINDOW = 6


LOGIT_SCALE = 10.0
LOGIT_BIAS = -3.0
LOSS_SCALE = 256.0
EPSILON = 1e-06


def shifted(value, axis, steps):
    count = lax.axis_size(axis)
    pairs = [(source, (source + steps) % count) for source in range(count)]
    return lax.ppermute(value, axis, pairs)


def unit_rows(values):
    values = values.astype(jnp.float32)
    inverse = lax.rsqrt(jnp.sum(values * values, axis=-1, keepdims=True) + EPSILON)
    return (values * inverse, inverse)


def pair_grad(images, texts, step_ids, col_ids, position):
    logits = (
        LOGIT_SCALE * jnp.einsum("ie,ke->ik", images, texts, preferred_element_type=jnp.float32)
        + LOGIT_BIAS
    )
    columns = lax.broadcasted_iota(jnp.int32, logits.shape, 1)
    positive = (step_ids[:, None] == position) & (col_ids[:, None] == columns)
    target = jnp.where(positive, 1.0, -1.0).astype(jnp.float32)
    return (-LOSS_SCALE * LOGIT_SCALE * target * jax.nn.sigmoid(-target * logits)).astype(
        jnp.bfloat16
    )


def shard_rows(table, shard, cycle_size, row_count):
    start = (shard + cycle_size) % cycle_size * row_count
    return lax.dynamic_slice_in_dim(table, start, row_count)


def move_block(travel, hop):
    return shifted(travel, "dp", hop)


def local(image_embeds, text_features, projection, pair_step, pair_col):
    cycle_size = lax.axis_size("dp")
    my_index = lax.axis_index("dp")
    row_count = image_embeds.shape[1]
    window_len = min(WINDOW, cycle_size)
    back_reach = window_len // 2 - 1
    unit_img = unit_rows(image_embeds[0])[0].astype(jnp.bfloat16)
    features = text_features[0]
    hidden = jnp.dot(features, projection, preferred_element_type=jnp.float32)
    unit_text, inverse_norm = unit_rows(hidden)
    text_units = unit_text.astype(jnp.bfloat16)
    all_steps = pair_step[0]
    all_cols = pair_col[0]
    streams = [(-back_reach, 0)] + [(1, position) for position in range(1, window_len)]
    my_steps = shard_rows(all_steps, my_index, cycle_size, row_count)
    my_cols = shard_rows(all_cols, my_index, cycle_size, row_count)
    travel = text_units
    running = None
    for hop, position in streams:
        travel = move_block(travel, hop)
        if running is not None:
            running = shifted(running.astype(jnp.bfloat16), "dp", hop).astype(running.dtype)
        weights = pair_grad(unit_img, travel, my_steps, my_cols, position)
        contribution = jnp.einsum(
            "ik,ie->ke", weights, unit_img, preferred_element_type=jnp.float32
        )
        running = contribution if running is None else running + contribution
    unit_grad = shifted(running.astype(jnp.bfloat16), "dp", back_reach - streams[-1][1]).astype(
        running.dtype
    )
    radial = jnp.sum(unit_text * unit_grad, axis=-1, keepdims=True)
    hidden_grad = (inverse_norm * (unit_grad - unit_text * radial)).astype(jnp.bfloat16)
    grad_text = jnp.einsum(
        "ke,de->kd", hidden_grad, projection, preferred_element_type=jnp.float32
    ).astype(jnp.bfloat16)
    partial_value = jnp.einsum(
        "kd,ke->de", features, hidden_grad, preferred_element_type=jnp.float32
    )
    partial_value = lax.optimization_barrier(partial_value.astype(jnp.bfloat16)).astype(jnp.float32)
    pooled = lax.psum_scatter(
        partial_value.astype(jnp.bfloat16), "outer", scatter_dimension=1, tiled=True
    ).astype(jnp.float32)
    owned = lax.psum_scatter(pooled, "dp", scatter_dimension=0, tiled=True)
    global_sq = lax.psum(jnp.sum(owned * owned), ("dp", "outer"))
    threshold = math.sqrt(projection.shape[0] * projection.shape[1])
    factor = jnp.minimum(1.0, threshold / jnp.sqrt(global_sq))
    return (grad_text[None], owned * factor)


CHUNKS = 4
LANES = 128
Z_SIZE = 4
QUAD = 4


def rows_ds(start, count):
    return pl.ds(pl.multiple_of(start, 16), count)


def kernel(
    image_hbm, text_hbm, proj_hbm, step_hbm, col_hbm,
    grad_text_ref, grad_proj_ref,
    image_ref, text_ref, proj_ref, step_ref, col_ref, load_sem,
    img, ftq, hs, hq, unit_text, inv_norm, units, ugrad, hgrad,
    psend, prec, own_part, zsend, zrec, sq_src, sq_quad, sq_mid, sq_dp,
    up_sem, down_sem, side_sem, side_two_sem, pass_sem, img_recv, ft_send, ft_recv, h_send, h_recv,
    p_send, p_recv, z_send, z_recv, q_send, q_recv, d_send, d_recv,
):
    bf16, f32 = jnp.bfloat16, jnp.float32
    me = lax.axis_index("dp")
    quad = lax.axis_index("outer")
    n_dp = 2 * Z_SIZE
    z, x = me // 2, me % 2
    rows, width = image_ref.shape
    chunk = rows // CHUNKS
    own_rows, own_cols = grad_proj_ref.shape

    def device(dp, outer):
        return {"dp": dp, "outer": outer}

    loads = [
        pltpu.make_async_copy(source, target, load_sem.at[i])
        for i, (source, target) in enumerate((
            (image_hbm.at[0], image_ref), (text_hbm.at[0], text_ref), (proj_hbm, proj_ref),
            (step_hbm, step_ref), (col_hbm, col_ref)))
    ]
    for load in loads:
        load.start()

    barrier = pltpu.get_barrier_semaphore()
    for i in range(1, QUAD):
        pl.semaphore_signal(barrier, inc=1, device_id=device(me, (quad + i) % QUAD),
                            device_id_type=pl.DeviceIdType.MESH)
    for i in range(1, n_dp):
        pl.semaphore_signal(barrier, inc=1, device_id=device((me + i) % n_dp, quad),
                            device_id_type=pl.DeviceIdType.MESH)

    loads[0].wait()
    values = image_ref[...].astype(f32)
    inverse = lax.rsqrt(jnp.sum(values * values, axis=-1, keepdims=True) + EPSILON)
    img[me] = (values * inverse).astype(bf16)
    pl.semaphore_wait(barrier, QUAD - 1 + n_dp - 1)

    def image_copy(block, part, target, send_sem):
        where = img.at[block, pl.ds(part * chunk, chunk)]
        return pltpu.make_async_remote_copy(
            src_ref=where, dst_ref=where, send_sem=send_sem, recv_sem=img_recv.at[block, part],
            device_id=device(target, quad), device_id_type=pl.DeviceIdType.MESH)

    ahead, behind = (z + 1) % Z_SIZE, (z + Z_SIZE - 1) % Z_SIZE
    partner = me + 1 - 2 * x
    col_ahead, col_behind = 2 * ahead + x, 2 * behind + x
    side_ahead = 2 * ahead + 1 - x
    third = jnp.where(x == 0, 2 * behind + 1, 2 * ((z + 2) % Z_SIZE))
    passed = jnp.where(x == 0, me + 1, 2 * ahead)
    passed_to = jnp.where(x == 0, col_ahead, col_behind)

    def own_copies(part):
        return (
            image_copy(me, part, col_ahead, up_sem.at[part]),
            image_copy(me, part, col_behind, down_sem.at[part]),
            image_copy(me, part, partner, side_sem.at[part]),
        )

    def side_copy(part):
        return image_copy(col_ahead, part, partner, side_two_sem.at[part])

    def passed_copy(part):
        return image_copy(passed, part, passed_to, pass_sem.at[part])

    def arrived(block, part):
        image_copy(block, part, partner, side_sem.at[part]).wait_recv()

    for part in range(CHUNKS):
        for copy in own_copies(part):
            copy.start()

    loads[1].wait()
    turned = text_ref[...].astype(f32).T
    for zc in range(Z_SIZE):
        for xc in range(2):
            at = (2 * zc + xc) * own_rows
            ftq[quad, pl.ds((xc * Z_SIZE + zc) * own_rows, own_rows)] = (
                turned[at:at + own_rows].astype(bf16))

    def ft_copy(source, i):
        return pltpu.make_async_remote_copy(
            src_ref=ftq.at[source], dst_ref=ftq.at[source], send_sem=ft_send.at[i],
            recv_sem=ft_recv.at[source], device_id=device(me, (quad + i) % QUAD),
            device_id_type=pl.DeviceIdType.MESH)

    for i in range(1, QUAD):
        ft_copy(quad, i).start()

    loads[2].wait()
    hidden = jnp.dot(text_ref[...], proj_ref[...], preferred_element_type=f32)
    inv = lax.rsqrt(jnp.sum(hidden * hidden, axis=-1, keepdims=True) + EPSILON)
    inv_norm[...] = jnp.broadcast_to(inv, inv_norm.shape)
    unit = hidden * inv
    unit_text[...] = unit
    units[...] = unit.astype(bf16)
    loads[3].wait()
    loads[4].wait()

    def pair_step(block, parts, first=False):
        position = (block - me + 2 + n_dp) % n_dp
        start, count = parts[0] * chunk, len(parts) * chunk
        images = img[block, pl.ds(start, count)]
        dots = lax.dot_general(units[...], images, (((1,), (1,)), ((), ())),
                               preferred_element_type=f32)
        logits = LOGIT_SCALE * dots + LOGIT_BIAS
        columns = lax.broadcasted_iota(jnp.int32, logits.shape, 0)
        where = pl.ds(pl.multiple_of(block * rows + start, LANES), count)
        positive = jnp.logical_and(step_ref[:, where] == position, col_ref[:, where] == columns)
        target = jnp.where(positive, 1.0, -1.0).astype(f32)
        weights = (-LOSS_SCALE * LOGIT_SCALE * target * jax.nn.sigmoid(-target * logits)).astype(bf16)
        term = jnp.dot(weights, images, preferred_element_type=f32)
        if first:
            ugrad[...] = term
        else:
            ugrad[...] += term

    every = range(CHUNKS)
    halves = (every[:CHUNKS // 2], every[CHUNKS // 2:])
    pair_step(me, every, first=True)
    for part in every:
        arrived(col_ahead, part)
        side_copy(part).start()
        arrived(partner, part)

        @pl.when(x == 0)
        def _():
            passed_copy(part).start()

    pair_step(partner, every)
    pair_step(col_ahead, every)
    for part in every:
        arrived(col_behind, part)
    pair_step(col_behind, every)
    for parts in halves:
        for part in parts:
            arrived(side_ahead, part)

            @pl.when(x == 1)
            def _():
                passed_copy(part).start()

        pair_step(side_ahead, parts)
    for parts in halves:
        for part in parts:
            arrived(third, part)
        pair_step(third, parts)

    unit = unit_text[...]
    total = ugrad[...]
    radial = jnp.sum(unit * total, axis=-1, keepdims=True)
    hidden_grad = (inv_norm[:, :1] * (total - unit * radial)).astype(bf16)
    hgrad[...] = hidden_grad
    wide = hidden_grad.astype(f32)
    slices = -(-own_cols // LANES)
    for c in range(QUAD):
        moved = wide if c == 0 else pltpu.roll(wide, width - c * own_cols, 1)
        for s in range(slices):
            hs[c, s] = moved[:, s * LANES:(s + 1) * LANES].astype(bf16)

    def h_copy(source, i, s):
        return pltpu.make_async_remote_copy(
            src_ref=hs.at[(quad + i) % QUAD, s], dst_ref=hq.at[source, s],
            send_sem=h_send.at[i, s], recv_sem=h_recv.at[source, s],
            device_id=device(me, (quad + i) % QUAD), device_id_type=pl.DeviceIdType.MESH)

    for s in range(slices):
        for i in range(1, QUAD):
            h_copy(quad, i, s).start()
    hq[quad] = hs[quad]
    grad_text_ref[0] = lax.dot_general(
        hgrad[...], proj_ref[...], (((1,), (1,)), ((), ())), preferred_element_type=f32
    ).astype(bf16)

    for i in range(1, QUAD):
        ft_copy((quad + i) % QUAD, i).wait_recv()

    half = Z_SIZE * own_rows

    def half_sum(which, s):
        acc = None
        for q in range(QUAD):
            term = jnp.dot(ftq[q, rows_ds(which * half, half)], hq[q, s],
                           preferred_element_type=f32)
            acc = term if acc is None else acc + term
        return acc

    def p_copy(zc, s):
        return pltpu.make_async_remote_copy(
            src_ref=psend.at[s, zc], dst_ref=prec.at[s, zc], send_sem=p_send.at[zc, s],
            recv_sem=p_recv.at[zc, s], device_id=device(partner, quad),
            device_id_type=pl.DeviceIdType.MESH)

    def z_copy(source, i, s):
        return pltpu.make_async_remote_copy(
            src_ref=zsend.at[s, i], dst_ref=zrec.at[s, source], send_sem=z_send.at[i, s],
            recv_sem=z_recv.at[source, s], device_id=device((me + 2 * i) % n_dp, quad),
            device_id_type=pl.DeviceIdType.MESH)

    def send_half(s):
        for i in range(1, QUAD):
            h_copy((quad + i) % QUAD, i, s).wait_recv()
        part_sum = half_sum(1 - x, s)
        for zc in range(Z_SIZE):
            psend[s, zc] = part_sum[zc * own_rows:(zc + 1) * own_rows].astype(bf16)
            p_copy(zc, s).start()
        part_sum = half_sum(x, s)
        for zc in range(Z_SIZE):
            own_part[s, zc] = part_sum[zc * own_rows:(zc + 1) * own_rows]

    def send_owners(s):
        for i in (2, 1, 3):
            to = (z + i) % Z_SIZE
            p_copy(to, s).wait_recv()
            zsend[s, i] = (own_part[s, to] + prec[s, to].astype(f32)).astype(bf16)
            z_copy(z, i, s).start()

    def finished(s):
        p_copy(z, s).wait_recv()
        owned = own_part[s, z] + prec[s, z].astype(f32)
        for i in range(1, Z_SIZE):
            source = (z + i) % Z_SIZE
            z_copy(source, i, s).wait_recv()
            owned = owned + zrec[s, source].astype(f32)
        lanes = lax.broadcasted_iota(jnp.int32, owned.shape, 1)
        return jnp.where(lanes < own_cols - s * LANES, owned, 0.0)

    for s in range(slices):
        send_half(s)
        if s > 0:
            send_owners(s - 1)
    send_owners(slices - 1)
    owned = [finished(s) for s in range(slices)]
    squares = owned[0] * owned[0]
    for piece in owned[1:]:
        squares = squares + piece * piece
    sq_src[...] = jnp.broadcast_to(jnp.sum(squares), sq_src.shape)

    def q_copy(source, i):
        return pltpu.make_async_remote_copy(
            src_ref=sq_src, dst_ref=sq_quad.at[source], send_sem=q_send.at[i],
            recv_sem=q_recv.at[source], device_id=device(me, (quad + i) % QUAD),
            device_id_type=pl.DeviceIdType.MESH)

    def d_copy(source, i):
        return pltpu.make_async_remote_copy(
            src_ref=sq_mid, dst_ref=sq_dp.at[source], send_sem=d_send.at[i],
            recv_sem=d_recv.at[source], device_id=device((me + i) % n_dp, quad),
            device_id_type=pl.DeviceIdType.MESH)

    for i in range(1, QUAD):
        q_copy(quad, i).start()
    sq_quad[quad] = sq_src[...]
    for i in range(1, QUAD):
        q_copy((quad + i) % QUAD, i).wait_recv()
    sq_mid[...] = sq_quad[0] + sq_quad[1] + sq_quad[2] + sq_quad[3]
    for i in range(1, n_dp):
        d_copy(me, i).start()
    sq_dp[me] = sq_mid[...]

    for part in range(CHUNKS):
        for copy in (*own_copies(part), side_copy(part), passed_copy(part)):
            copy.wait_send()
    for i in range(1, QUAD):
        ft_copy(quad, i).wait_send()
        for s in range(slices):
            h_copy(quad, i, s).wait_send()
        q_copy(quad, i).wait_send()
    for s in range(slices):
        for zc in range(Z_SIZE):
            p_copy(zc, s).wait_send()
        for i in range(1, Z_SIZE):
            z_copy(z, i, s).wait_send()

    for i in range(1, n_dp):
        d_copy((me + i) % n_dp, i).wait_recv()
    global_sq = sq_dp[0]
    for i in range(1, n_dp):
        global_sq = global_sq + sq_dp[i]
    threshold = math.sqrt(width * proj_ref.shape[0])
    factor = jnp.minimum(1.0, threshold / jnp.sqrt(global_sq[:1, :1]))
    for s in range(slices):
        count = min(LANES, own_cols - s * LANES)
        grad_proj_ref[:, s * LANES:s * LANES + count] = owned[s][:, :count] * factor
    for i in range(1, n_dp):
        d_copy(me, i).wait_send()


def fused(image_embeds, text_features, projection, pair_step, pair_col):
    n_dp, n_outer = lax.axis_size("dp"), lax.axis_size("outer")
    rows, width = image_embeds.shape[1:]
    depth = projection.shape[0]
    own_rows, own_cols = depth // n_dp, width // n_outer
    bf16, f32 = jnp.bfloat16, jnp.float32
    dma = pltpu.SemaphoreType.DMA
    vmem = pl.BlockSpec(memory_space=pltpu.VMEM)
    anywhere = pl.BlockSpec(memory_space=pl.ANY)
    slices = -(-own_cols // LANES)
    slab = (own_rows, LANES)
    grad_text, grad_proj = pl.pallas_call(
        kernel,
        out_shape=(
            jax.ShapeDtypeStruct((1, rows, depth), bf16),
            jax.ShapeDtypeStruct((own_rows, own_cols), f32),
        ),
        in_specs=[anywhere] * 5,
        out_specs=(vmem, vmem),
        scratch_shapes=[
            pltpu.VMEM((rows, width), bf16),
            pltpu.VMEM((rows, depth), bf16),
            pltpu.VMEM((depth, width), bf16),
            pltpu.VMEM((1, n_dp * rows), jnp.int32),
            pltpu.VMEM((1, n_dp * rows), jnp.int32),
            dma((5,)),
            pltpu.VMEM((n_dp, rows, width), bf16),
            pltpu.VMEM((QUAD, depth, rows), bf16),
            pltpu.VMEM((QUAD, slices, rows, LANES), bf16),
            pltpu.VMEM((QUAD, slices, rows, LANES), bf16),
            pltpu.VMEM((rows, width), f32),
            pltpu.VMEM((rows, 128), f32),
            pltpu.VMEM((rows, width), bf16),
            pltpu.VMEM((rows, width), f32),
            pltpu.VMEM((rows, width), bf16),
            pltpu.VMEM((slices, Z_SIZE, *slab), bf16),
            pltpu.VMEM((slices, Z_SIZE, *slab), bf16),
            pltpu.VMEM((slices, Z_SIZE, *slab), f32),
            pltpu.VMEM((slices, Z_SIZE, *slab), bf16),
            pltpu.VMEM((slices, Z_SIZE, *slab), bf16),
            pltpu.VMEM((8, 128), f32),
            pltpu.VMEM((QUAD, 8, 128), f32),
            pltpu.VMEM((8, 128), f32),
            pltpu.VMEM((n_dp, 8, 128), f32),
            dma((CHUNKS,)), dma((CHUNKS,)), dma((CHUNKS,)), dma((CHUNKS,)), dma((CHUNKS,)),
            dma((n_dp, CHUNKS)),
            dma((QUAD,)), dma((QUAD,)), dma((QUAD, slices)), dma((QUAD, slices)),
            dma((Z_SIZE, slices)), dma((Z_SIZE, slices)),
            dma((Z_SIZE, slices)), dma((Z_SIZE, slices)),
            dma((QUAD,)), dma((QUAD,)), dma((n_dp,)), dma((n_dp,)),
        ],
        compiler_params=pltpu.CompilerParams(
            collective_id=0, has_side_effects=True, vmem_limit_bytes=60 * 1024 * 1024
        ),
        cost_estimate=pl.CostEstimate(
            flops=2 * rows * depth * width * 3 + 4 * WINDOW * rows * rows * width,
            bytes_accessed=2 * (4 * rows * width + depth * width),
            transcendentals=WINDOW * rows * rows,
        ),
    )(
        image_embeds, text_features, projection, pair_step, pair_col
    )
    return pl.pallas_call(
        copy_out,
        out_shape=(
            jax.ShapeDtypeStruct(grad_text.shape, bf16), jax.ShapeDtypeStruct(grad_proj.shape, f32)
        ),
        in_specs=[anywhere] * 2,
        out_specs=(anywhere, anywhere),
        scratch_shapes=[dma((2,))],
        compiler_params=pltpu.CompilerParams(vmem_limit_bytes=60 * 1024 * 1024),
    )(grad_text, grad_proj)


def copy_out(text_from, proj_from, text_to, proj_to, sems):
    copies = (
        pltpu.make_async_copy(text_from, text_to, sems.at[0]),
        pltpu.make_async_copy(proj_from, proj_to, sems.at[1]),
    )
    for copy in copies:
        copy.start()
    for copy in copies:
        copy.wait()


def solution(mesh):
    placed = (
        P("outer", "dp", None),
        P("outer", "dp", None),
        P(),
        P("outer", None),
        P("outer", None),
    )
    small = mesh.shape["dp"] == 2 * Z_SIZE and mesh.shape["outer"] == QUAD
    return jax.shard_map(
        fused if small else local,
        mesh=mesh,
        in_specs=placed,
        out_specs=(P("outer", "dp", None), P("dp", "outer")),
        check_vma=False,
    )
```

```python
import math

import jax
import jax.numpy as jnp
from jax import lax
from jax.experimental import pallas as pl
from jax.experimental.pallas import tpu as pltpu
from jax.sharding import PartitionSpec as P

WINDOW = 6


LOGIT_SCALE = 10.0
LOGIT_BIAS = -3.0
LOSS_SCALE = 256.0
EPSILON = 1e-06


def shifted(value, axis, steps):
    count = lax.axis_size(axis)
    pairs = [(source, (source + steps) % count) for source in range(count)]
    return lax.ppermute(value, axis, pairs)


def unit_rows(values):
    values = values.astype(jnp.float32)
    inverse = lax.rsqrt(jnp.sum(values * values, axis=-1, keepdims=True) + EPSILON)
    return (values * inverse, inverse)


def pair_grad(images, texts, step_ids, col_ids, position):
    logits = (
        LOGIT_SCALE * jnp.einsum("ie,ke->ik", images, texts, preferred_element_type=jnp.float32)
        + LOGIT_BIAS
    )
    columns = lax.broadcasted_iota(jnp.int32, logits.shape, 1)
    positive = (step_ids[:, None] == position) & (col_ids[:, None] == columns)
    target = jnp.where(positive, 1.0, -1.0).astype(jnp.float32)
    return (-LOSS_SCALE * LOGIT_SCALE * target * jax.nn.sigmoid(-target * logits)).astype(
        jnp.bfloat16
    )


def shard_rows(table, shard, cycle_size, row_count):
    start = (shard + cycle_size) % cycle_size * row_count
    return lax.dynamic_slice_in_dim(table, start, row_count)


def move_block(travel, hop):
    return shifted(travel, "dp", hop)


def local(image_embeds, text_features, projection, pair_step, pair_col):
    cycle_size = lax.axis_size("dp")
    my_index = lax.axis_index("dp")
    row_count = image_embeds.shape[1]
    window_len = min(WINDOW, cycle_size)
    back_reach = window_len // 2 - 1
    unit_img = unit_rows(image_embeds[0])[0].astype(jnp.bfloat16)
    features = text_features[0]
    hidden = jnp.dot(features, projection, preferred_element_type=jnp.float32)
    unit_text, inverse_norm = unit_rows(hidden)
    text_units = unit_text.astype(jnp.bfloat16)
    all_steps = pair_step[0]
    all_cols = pair_col[0]
    streams = [(-back_reach, 0)] + [(1, position) for position in range(1, window_len)]
    my_steps = shard_rows(all_steps, my_index, cycle_size, row_count)
    my_cols = shard_rows(all_cols, my_index, cycle_size, row_count)
    travel = text_units
    running = None
    for hop, position in streams:
        travel = move_block(travel, hop)
        if running is not None:
            running = shifted(running.astype(jnp.bfloat16), "dp", hop).astype(running.dtype)
        weights = pair_grad(unit_img, travel, my_steps, my_cols, position)
        contribution = jnp.einsum(
            "ik,ie->ke", weights, unit_img, preferred_element_type=jnp.float32
        )
        running = contribution if running is None else running + contribution
    unit_grad = shifted(running.astype(jnp.bfloat16), "dp", back_reach - streams[-1][1]).astype(
        running.dtype
    )
    radial = jnp.sum(unit_text * unit_grad, axis=-1, keepdims=True)
    hidden_grad = (inverse_norm * (unit_grad - unit_text * radial)).astype(jnp.bfloat16)
    grad_text = jnp.einsum(
        "ke,de->kd", hidden_grad, projection, preferred_element_type=jnp.float32
    ).astype(jnp.bfloat16)
    partial_value = jnp.einsum(
        "kd,ke->de", features, hidden_grad, preferred_element_type=jnp.float32
    )
    partial_value = lax.optimization_barrier(partial_value.astype(jnp.bfloat16)).astype(jnp.float32)
    pooled = lax.psum_scatter(
        partial_value.astype(jnp.bfloat16), "outer", scatter_dimension=1, tiled=True
    ).astype(jnp.float32)
    owned = lax.psum_scatter(pooled, "dp", scatter_dimension=0, tiled=True)
    global_sq = lax.psum(jnp.sum(owned * owned), ("dp", "outer"))
    threshold = math.sqrt(projection.shape[0] * projection.shape[1])
    factor = jnp.minimum(1.0, threshold / jnp.sqrt(global_sq))
    return (grad_text[None], owned * factor)


CHUNKS = 4
LANES = 128
Z_SIZE = 4
QUAD = 4


def rows_ds(start, count):
    return pl.ds(pl.multiple_of(start, 16), count)


def kernel(
    image_hbm, text_hbm, proj_hbm, step_hbm, col_hbm,
    grad_text_ref, grad_proj_ref,
    image_ref, text_ref, proj_ref, step_ref, col_ref, load_sem,
    img, ftq, hs, hq, unit_text, inv_norm, units, ugrad, hgrad,
    psend, prec, own_part, zsend, zrec, sq_src, sq_quad, sq_mid, sq_dp,
    up_sem, down_sem, side_sem, side_two_sem, pass_sem, img_recv, ft_send, ft_recv, h_send, h_recv,
    p_send, p_recv, z_send, z_recv, q_send, q_recv, d_send, d_recv,
):
    bf16, f32 = jnp.bfloat16, jnp.float32
    me = lax.axis_index("dp")
    quad = lax.axis_index("outer")
    n_dp = 2 * Z_SIZE
    z, x = me // 2, me % 2
    rows, width = image_ref.shape
    chunk = rows // CHUNKS
    own_rows, own_cols = grad_proj_ref.shape

    def device(dp, outer):
        return {"dp": dp, "outer": outer}

    loads = [
        pltpu.make_async_copy(source, target, load_sem.at[i])
        for i, (source, target) in enumerate((
            (image_hbm.at[0], image_ref), (text_hbm.at[0], text_ref), (proj_hbm, proj_ref),
            (step_hbm, step_ref), (col_hbm, col_ref)))
    ]
    for load in loads:
        load.start()

    barrier = pltpu.get_barrier_semaphore()
    for i in range(1, QUAD):
        pl.semaphore_signal(barrier, inc=1, device_id=device(me, (quad + i) % QUAD),
                            device_id_type=pl.DeviceIdType.MESH)
    for i in range(1, n_dp):
        pl.semaphore_signal(barrier, inc=1, device_id=device((me + i) % n_dp, quad),
                            device_id_type=pl.DeviceIdType.MESH)

    loads[0].wait()
    values = image_ref[...].astype(f32)
    inverse = lax.rsqrt(jnp.sum(values * values, axis=-1, keepdims=True) + EPSILON)
    img[me] = (values * inverse).astype(bf16)
    pl.semaphore_wait(barrier, QUAD - 1 + n_dp - 1)

    def image_copy(block, part, target, send_sem):
        where = img.at[block, pl.ds(part * chunk, chunk)]
        return pltpu.make_async_remote_copy(
            src_ref=where, dst_ref=where, send_sem=send_sem, recv_sem=img_recv.at[block, part],
            device_id=device(target, quad), device_id_type=pl.DeviceIdType.MESH)

    ahead, behind = (z + 1) % Z_SIZE, (z + Z_SIZE - 1) % Z_SIZE
    partner = me + 1 - 2 * x
    col_ahead, col_behind = 2 * ahead + x, 2 * behind + x
    side_ahead = 2 * ahead + 1 - x
    third = jnp.where(x == 0, 2 * behind + 1, 2 * ((z + 2) % Z_SIZE))
    passed = jnp.where(x == 0, me + 1, 2 * ahead)
    passed_to = jnp.where(x == 0, col_ahead, col_behind)

    def own_copies(part):
        return (
            image_copy(me, part, col_ahead, up_sem.at[part]),
            image_copy(me, part, col_behind, down_sem.at[part]),
            image_copy(me, part, partner, side_sem.at[part]),
        )

    def side_copy(part):
        return image_copy(col_ahead, part, partner, side_two_sem.at[part])

    def passed_copy(part):
        return image_copy(passed, part, passed_to, pass_sem.at[part])

    def arrived(block, part):
        image_copy(block, part, partner, side_sem.at[part]).wait_recv()

    for part in range(CHUNKS):
        for copy in own_copies(part):
            copy.start()

    loads[1].wait()
    turned = text_ref[...].astype(f32).T
    for zc in range(Z_SIZE):
        for xc in range(2):
            at = (2 * zc + xc) * own_rows
            ftq[quad, pl.ds((xc * Z_SIZE + zc) * own_rows, own_rows)] = (
                turned[at:at + own_rows].astype(bf16))

    def ft_copy(source, i):
        return pltpu.make_async_remote_copy(
            src_ref=ftq.at[source], dst_ref=ftq.at[source], send_sem=ft_send.at[i],
            recv_sem=ft_recv.at[source], device_id=device(me, (quad + i) % QUAD),
            device_id_type=pl.DeviceIdType.MESH)

    for i in range(1, QUAD):
        ft_copy(quad, i).start()

    loads[2].wait()
    hidden = jnp.dot(text_ref[...], proj_ref[...], preferred_element_type=f32)
    inv = lax.rsqrt(jnp.sum(hidden * hidden, axis=-1, keepdims=True) + EPSILON)
    inv_norm[...] = jnp.broadcast_to(inv, inv_norm.shape)
    unit = hidden * inv
    unit_text[...] = unit
    units[...] = unit.astype(bf16)
    loads[3].wait()
    loads[4].wait()

    def pair_step(block, parts, first=False):
        position = (block - me + 2 + n_dp) % n_dp
        start, count = parts[0] * chunk, len(parts) * chunk
        images = img[block, pl.ds(start, count)]
        dots = lax.dot_general(units[...], images, (((1,), (1,)), ((), ())),
                               preferred_element_type=f32)
        logits = LOGIT_SCALE * dots + LOGIT_BIAS
        columns = lax.broadcasted_iota(jnp.int32, logits.shape, 0)
        where = pl.ds(pl.multiple_of(block * rows + start, LANES), count)
        positive = jnp.logical_and(step_ref[:, where] == position, col_ref[:, where] == columns)
        target = jnp.where(positive, 1.0, -1.0).astype(f32)
        weights = (-LOSS_SCALE * LOGIT_SCALE * target * jax.nn.sigmoid(-target * logits)).astype(bf16)
        term = jnp.dot(weights, images, preferred_element_type=f32)
        if first:
            ugrad[...] = term
        else:
            ugrad[...] += term

    every = range(CHUNKS)
    halves = (every[:CHUNKS // 2], every[CHUNKS // 2:])
    pair_step(me, every, first=True)
    for part in every:
        arrived(col_ahead, part)
        side_copy(part).start()
        arrived(partner, part)

        @pl.when(x == 0)
        def _():
            passed_copy(part).start()

    pair_step(partner, every)
    pair_step(col_ahead, every)
    for part in every:
        arrived(col_behind, part)
    pair_step(col_behind, every)
    for parts in halves:
        for part in parts:
            arrived(side_ahead, part)

            @pl.when(x == 1)
            def _():
                passed_copy(part).start()

        pair_step(side_ahead, parts)
    for parts in halves:
        for part in parts:
            arrived(third, part)
        pair_step(third, parts)

    unit = unit_text[...]
    total = ugrad[...]
    radial = jnp.sum(unit * total, axis=-1, keepdims=True)
    hidden_grad = (inv_norm[:, :1] * (total - unit * radial)).astype(bf16)
    hgrad[...] = hidden_grad
    wide = hidden_grad.astype(f32)
    slices = -(-own_cols // LANES)
    for c in range(QUAD):
        moved = wide if c == 0 else pltpu.roll(wide, width - c * own_cols, 1)
        for s in range(slices):
            hs[c, s] = moved[:, s * LANES:(s + 1) * LANES].astype(bf16)

    def h_copy(source, i, s):
        return pltpu.make_async_remote_copy(
            src_ref=hs.at[(quad + i) % QUAD, s], dst_ref=hq.at[source, s],
            send_sem=h_send.at[i, s], recv_sem=h_recv.at[source, s],
            device_id=device(me, (quad + i) % QUAD), device_id_type=pl.DeviceIdType.MESH)

    for s in range(slices):
        for i in range(1, QUAD):
            h_copy(quad, i, s).start()
    hq[quad] = hs[quad]
    grad_text_ref[0] = lax.dot_general(
        hgrad[...], proj_ref[...], (((1,), (1,)), ((), ())), preferred_element_type=f32
    ).astype(bf16)

    for i in range(1, QUAD):
        ft_copy((quad + i) % QUAD, i).wait_recv()

    half = Z_SIZE * own_rows

    def half_sum(which, s):
        acc = None
        for q in range(QUAD):
            term = jnp.dot(ftq[q, rows_ds(which * half, half)], hq[q, s],
                           preferred_element_type=f32)
            acc = term if acc is None else acc + term
        return acc

    def p_copy(zc, s):
        return pltpu.make_async_remote_copy(
            src_ref=psend.at[s, zc], dst_ref=prec.at[s, zc], send_sem=p_send.at[zc, s],
            recv_sem=p_recv.at[zc, s], device_id=device(partner, quad),
            device_id_type=pl.DeviceIdType.MESH)

    def z_copy(source, i, s):
        return pltpu.make_async_remote_copy(
            src_ref=zsend.at[s, i], dst_ref=zrec.at[s, source], send_sem=z_send.at[i, s],
            recv_sem=z_recv.at[source, s], device_id=device((me + 2 * i) % n_dp, quad),
            device_id_type=pl.DeviceIdType.MESH)

    def send_half(s):
        for i in range(1, QUAD):
            h_copy((quad + i) % QUAD, i, s).wait_recv()
        part_sum = half_sum(1 - x, s)
        for zc in range(Z_SIZE):
            psend[s, zc] = part_sum[zc * own_rows:(zc + 1) * own_rows].astype(bf16)
            p_copy(zc, s).start()
        part_sum = half_sum(x, s)
        for zc in range(Z_SIZE):
            own_part[s, zc] = part_sum[zc * own_rows:(zc + 1) * own_rows]

    def send_owners(s):
        for i in (2, 1, 3):
            to = (z + i) % Z_SIZE
            p_copy(to, s).wait_recv()
            zsend[s, i] = (own_part[s, to] + prec[s, to].astype(f32)).astype(bf16)
            z_copy(z, i, s).start()

    def finished(s):
        p_copy(z, s).wait_recv()
        owned = own_part[s, z] + prec[s, z].astype(f32)
        for i in range(1, Z_SIZE):
            source = (z + i) % Z_SIZE
            z_copy(source, i, s).wait_recv()
            owned = owned + zrec[s, source].astype(f32)
        lanes = lax.broadcasted_iota(jnp.int32, owned.shape, 1)
        return jnp.where(lanes < own_cols - s * LANES, owned, 0.0)

    for s in range(slices):
        send_half(s)
        if s > 0:
            send_owners(s - 1)
    send_owners(slices - 1)
    owned = [finished(s) for s in range(slices)]
    squares = owned[0] * owned[0]
    for piece in owned[1:]:
        squares = squares + piece * piece
    sq_src[...] = jnp.broadcast_to(jnp.sum(squares), sq_src.shape)

    def q_copy(source, i):
        return pltpu.make_async_remote_copy(
            src_ref=sq_src, dst_ref=sq_quad.at[source], send_sem=q_send.at[i],
            recv_sem=q_recv.at[source], device_id=device(me, (quad + i) % QUAD),
            device_id_type=pl.DeviceIdType.MESH)

    def d_copy(source, i):
        return pltpu.make_async_remote_copy(
            src_ref=sq_mid, dst_ref=sq_dp.at[source], send_sem=d_send.at[i],
            recv_sem=d_recv.at[source], device_id=device((me + i) % n_dp, quad),
            device_id_type=pl.DeviceIdType.MESH)

    for i in range(1, QUAD):
        q_copy(quad, i).start()
    sq_quad[quad] = sq_src[...]
    for i in range(1, QUAD):
        q_copy((quad + i) % QUAD, i).wait_recv()
    sq_mid[...] = sq_quad[0] + sq_quad[1] + sq_quad[2] + sq_quad[3]
    for i in range(1, n_dp):
        d_copy(me, i).start()
    sq_dp[me] = sq_mid[...]

    for part in range(CHUNKS):
        for copy in (*own_copies(part), side_copy(part), passed_copy(part)):
            copy.wait_send()
    for i in range(1, QUAD):
        ft_copy(quad, i).wait_send()
        for s in range(slices):
            h_copy(quad, i, s).wait_send()
        q_copy(quad, i).wait_send()
    for s in range(slices):
        for zc in range(Z_SIZE):
            p_copy(zc, s).wait_send()
        for i in range(1, Z_SIZE):
            z_copy(z, i, s).wait_send()

    for i in range(1, n_dp):
        d_copy((me + i) % n_dp, i).wait_recv()
    global_sq = sq_dp[0]
    for i in range(1, n_dp):
        global_sq = global_sq + sq_dp[i]
    threshold = math.sqrt(width * proj_ref.shape[0])
    factor = jnp.minimum(1.0, threshold / jnp.sqrt(global_sq[:1, :1]))
    for s in range(slices):
        count = min(LANES, own_cols - s * LANES)
        grad_proj_ref[:, s * LANES:s * LANES + count] = owned[s][:, :count] * factor
    for i in range(1, n_dp):
        d_copy(me, i).wait_send()


def fused(image_embeds, text_features, projection, pair_step, pair_col):
    n_dp, n_outer = lax.axis_size("dp"), lax.axis_size("outer")
    rows, width = image_embeds.shape[1:]
    depth = projection.shape[0]
    own_rows, own_cols = depth // n_dp, width // n_outer
    bf16, f32 = jnp.bfloat16, jnp.float32
    dma = pltpu.SemaphoreType.DMA
    vmem = pl.BlockSpec(memory_space=pltpu.VMEM)
    anywhere = pl.BlockSpec(memory_space=pl.ANY)
    slices = -(-own_cols // LANES)
    slab = (own_rows, LANES)
    grad_text, grad_proj = pl.pallas_call(
        kernel,
        out_shape=(
            jax.ShapeDtypeStruct((1, rows, depth), bf16),
            jax.ShapeDtypeStruct((own_rows, own_cols), f32),
        ),
        in_specs=[anywhere] * 5,
        out_specs=(vmem, vmem),
        scratch_shapes=[
            pltpu.VMEM((rows, width), bf16),
            pltpu.VMEM((rows, depth), bf16),
            pltpu.VMEM((depth, width), bf16),
            pltpu.VMEM((1, n_dp * rows), jnp.int32),
            pltpu.VMEM((1, n_dp * rows), jnp.int32),
            dma((5,)),
            pltpu.VMEM((n_dp, rows, width), bf16),
            pltpu.VMEM((QUAD, depth, rows), bf16),
            pltpu.VMEM((QUAD, slices, rows, LANES), bf16),
            pltpu.VMEM((QUAD, slices, rows, LANES), bf16),
            pltpu.VMEM((rows, width), f32),
            pltpu.VMEM((rows, 128), f32),
            pltpu.VMEM((rows, width), bf16),
            pltpu.VMEM((rows, width), f32),
            pltpu.VMEM((rows, width), bf16),
            pltpu.VMEM((slices, Z_SIZE, *slab), bf16),
            pltpu.VMEM((slices, Z_SIZE, *slab), bf16),
            pltpu.VMEM((slices, Z_SIZE, *slab), f32),
            pltpu.VMEM((slices, Z_SIZE, *slab), bf16),
            pltpu.VMEM((slices, Z_SIZE, *slab), bf16),
            pltpu.VMEM((8, 128), f32),
            pltpu.VMEM((QUAD, 8, 128), f32),
            pltpu.VMEM((8, 128), f32),
            pltpu.VMEM((n_dp, 8, 128), f32),
            dma((CHUNKS,)), dma((CHUNKS,)), dma((CHUNKS,)), dma((CHUNKS,)), dma((CHUNKS,)),
            dma((n_dp, CHUNKS)),
            dma((QUAD,)), dma((QUAD,)), dma((QUAD, slices)), dma((QUAD, slices)),
            dma((Z_SIZE, slices)), dma((Z_SIZE, slices)),
            dma((Z_SIZE, slices)), dma((Z_SIZE, slices)),
            dma((QUAD,)), dma((QUAD,)), dma((n_dp,)), dma((n_dp,)),
        ],
        compiler_params=pltpu.CompilerParams(
            collective_id=0, has_side_effects=True, vmem_limit_bytes=60 * 1024 * 1024
        ),
        cost_estimate=pl.CostEstimate(
            flops=2 * rows * depth * width * 3 + 4 * WINDOW * rows * rows * width,
            bytes_accessed=2 * (4 * rows * width + depth * width),
            transcendentals=WINDOW * rows * rows,
        ),
    )(
        image_embeds, text_features, projection, pair_step, pair_col
    )
    return pl.pallas_call(
        copy_out,
        out_shape=(
            jax.ShapeDtypeStruct(grad_text.shape, bf16), jax.ShapeDtypeStruct(grad_proj.shape, f32)
        ),
        in_specs=[vmem] * 2,
        out_specs=(vmem, vmem),
    )(grad_text, grad_proj)


def copy_out(text_from, proj_from, text_to, proj_to):
    text_to[...] = text_from[...]
    proj_to[...] = proj_from[...]


def solution(mesh):
    placed = (
        P("outer", "dp", None),
        P("outer", "dp", None),
        P(),
        P("outer", None),
        P("outer", None),
    )
    small = mesh.shape["dp"] == 2 * Z_SIZE and mesh.shape["outer"] == QUAD
    return jax.shard_map(
        fused if small else local,
        mesh=mesh,
        in_specs=placed,
        out_specs=(P("outer", "dp", None), P("dp", "outer")),
        check_vma=False,
    )
```
